32 devices in a mesh: ctx: 8 (over y, x, core), tp: 4 (over z).
Axes of the slice: x: 2, y: 2, z: 4, core: 2. Of those that a mesh axis runs over, the one named last changes fastest.
Arguments:
- queries: bfloat16 [1536, 1024], P('ctx', 'tp'), may hold values from -6 to 6
- key_proj: bfloat16 [1536, 1024], P('ctx', 'tp'), may hold values from -6 to 6
- value_proj: bfloat16 [1536, 1024], P('ctx', 'tp'), may hold values from -6 to 6
- filters: float32 [1024, 128], P('tp'), may hold values from -0.5 to 0.5
- offsets: int32 [1536], P('ctx'), may hold values from 0 to 767, as said below
- out_weight: bfloat16 [4096, 1024], P(None, 'tp'), may hold values from -0.1875 to 0.1875
- out_grads: bfloat16 [1536, 4096], P(('ctx', 'tp')), may hold values from -6 to 6
Outputs:
- grad_queries: bfloat16 [1536, 1024], P('ctx', 'tp')
- grad_keys: bfloat16 [1536, 1024], P('ctx', 'tp')
- grad_values: bfloat16 [1536, 1024], P('ctx', 'tp')
- grad_filters: float32 [1024, 128], P('tp')
- grad_weight: float32 [4096, 1024], P('ctx', 'tp')
The draws below stay inside these ranges and needn't reach their ends.
Inputs may be any that keep to these rules, and one draw needn't show every extreme that they name: offsets counts up by one along each document of the packed sequence and is 0 at a document's first token (always at token 0); a document holds 1 to 768 tokens, and some document holds exactly 768.
All inputs are finite; a program needn't handle non-finite values.
Results may differ from the reference program's by a relative error of at most 0.0051.
Values may be sent and summed in bfloat16 or wider, within the bound.
A program may use at most 64 MiB of HBM per device.

```python
import jax
import jax.numpy as jnp
from jax import lax

D = 4096
TAPS = 128
CHANNELS = 1024
TOKENS = 1536
DOC_MOST = 768


def draw_offsets(key, part):
    base = jax.random.fold_in(key, 7)
    first_key, second_key, third_key = jax.random.split(base, 3)
    long_docs = jax.random.randint(first_key, (TOKENS,), 1, DOC_MOST + 1, dtype=jnp.int32)
    short_docs = jax.random.randint(second_key, (TOKENS,), 1, 2 * TAPS + 1, dtype=jnp.int32)
    picker = jax.random.randint(third_key, (TOKENS,), 0, 2, dtype=jnp.int32)
    lengths = jnp.where(picker == 1, long_docs, short_docs)
    lengths = lengths.at[0].set(DOC_MOST)
    ends = jnp.cumsum(lengths)
    starts = ends - lengths
    marks = jnp.zeros((TOKENS,), jnp.int32).at[starts].set(1, mode='drop')
    positions = jnp.arange(TOKENS, dtype=jnp.int32)
    doc_first = lax.cummax(positions * marks, axis=0)
    return positions - doc_first


def raised(entries, rng, source, target, blocks, factor):
    def block_of(position):
        return (jnp.arange(entries.shape[position]) // (entries.shape[position] // blocks)).reshape((-1,) + (1,) * (entries.ndim - 1 - position))

    one_side = jax.random.permutation(rng, blocks)[block_of(target)]
    second = (block_of(target) + blocks // 2) % blocks
    return jnp.where((block_of(source) == one_side) | (block_of(source) == second), factor * entries, entries)


def block_levels(rng, dims, pieces, least, largest):
    def one(dim, shards_of):
        draws = jax.random.uniform(jax.random.fold_in(jax.random.fold_in(rng, 6), dim), (shards_of,), jnp.float32, least / len(pieces), largest / len(pieces))
        return jnp.repeat(jnp.exp(draws), dims[dim] // shards_of).reshape((-1,) + (1,) * (len(dims) - dim - 1))

    loudness = one(*pieces[0])
    for cut in pieces[1:]:
        loudness = loudness * one(*cut)
    return loudness


def centred(key, dims, deviation, bound, shards=(), held_as=jnp.bfloat16):
    level = block_levels(key, dims, shards, -0.22, 0.18) if shards else 1.0
    array = jax.random.normal(key, dims, jnp.float32) * deviation * level
    return jnp.minimum(jnp.maximum(array, -bound), bound).astype(held_as)


def noise_with(stream_key, extent, deviation, bound, pieces, heavy, held_as=jnp.bfloat16):
    entries = deviation * jax.random.normal(stream_key, extent, jnp.float32)
    if pieces:
        entries = entries * block_levels(stream_key, extent, pieces, -0.22, 0.18)
    return jnp.clip(raised(entries, jax.random.fold_in(stream_key, 3), *heavy), -bound, bound).astype(held_as)


def setup_inputs(seed: int = 0) -> dict:
    key_of = jax.random.split(jax.random.key(seed), 8)
    queries = centred(key_of[0], (TOKENS, CHANNELS), 1.0, 6.0, ((0, 8), (1, 4)))
    key_proj = centred(key_of[1], (TOKENS, CHANNELS), 1.0, 6.0, ((0, 8), (1, 4)))
    value_proj = centred(key_of[2], (TOKENS, CHANNELS), 1.0, 6.0, ((0, 8), (1, 4)))
    filters = centred(key_of[3], (CHANNELS, TAPS), TAPS ** -0.5, 0.5, ((0, 4),), jnp.float32)
    offsets = draw_offsets(jax.random.fold_in(key_of[7], 71), 0)
    out_weight = centred(key_of[5], (D, CHANNELS), CHANNELS ** -0.5, 0.1875, ((1, 4),))
    out_grads = noise_with(key_of[6], (TOKENS, D), 1.0, 6.0, ((0, 32),), (0, 1, 32, 2.75))
    return {"queries": queries, "key_proj": key_proj, "value_proj": value_proj, "filters": filters, "offsets": offsets, "out_weight": out_weight, "out_grads": out_grads}


def rounded(values):
    return lax.optimization_barrier(values.astype(jnp.bfloat16))


def reference(queries, key_proj, value_proj, filters, offsets, out_weight, out_grads):
    rim_rows = TAPS - 1
    grad_scale = float(TOKENS) ** -0.5
    keys_wide = key_proj.astype(jnp.float32)
    values_wide = value_proj.astype(jnp.float32)
    queries_wide = queries.astype(jnp.float32)
    product = rounded(keys_wide * values_wide).astype(jnp.float32)
    capped = jnp.minimum(offsets, rim_rows).astype(jnp.int32)
    padded_front = jnp.concatenate([jnp.zeros((rim_rows, CHANNELS), jnp.float32), product], axis=0)

    def forward_tap(lag_index, running):
        lag_index = lag_index.astype(jnp.int32)
        window = lax.dynamic_slice_in_dim(padded_front, rim_rows - lag_index, TOKENS, 0)
        coeff = lax.dynamic_slice_in_dim(filters, lag_index, 1, 1)[:, 0]
        return running + coeff * window * (capped >= lag_index)[:, None]

    filtered = lax.fori_loop(0, TAPS, forward_tap, jnp.zeros((TOKENS, CHANNELS), jnp.float32))
    mixed_rows = rounded(queries_wide * filtered)
    grad_mixed = jnp.dot(out_grads, out_weight, preferred_element_type=jnp.float32)
    grad_weight = jnp.dot(out_grads.T, mixed_rows, preferred_element_type=jnp.float32) * grad_scale
    grad_filtered = rounded(grad_mixed * queries_wide).astype(jnp.float32)
    grad_queries = (grad_mixed * filtered).astype(jnp.bfloat16)
    padded_back = jnp.concatenate([grad_filtered, jnp.zeros((rim_rows, CHANNELS), jnp.float32)], axis=0)
    cap_back = jnp.concatenate([capped, jnp.full((rim_rows,), -1, jnp.int32)], axis=0)

    def backward_tap(lag_index, running):
        lag_index = lag_index.astype(jnp.int32)
        window = lax.dynamic_slice_in_dim(padded_back, lag_index, TOKENS, 0)
        window_cap = lax.dynamic_slice_in_dim(cap_back, lag_index, TOKENS, 0)
        coeff = lax.dynamic_slice_in_dim(filters, lag_index, 1, 1)[:, 0]
        return running + coeff * window * (window_cap >= lag_index)[:, None]

    grad_product = lax.fori_loop(0, TAPS, backward_tap, jnp.zeros((TOKENS, CHANNELS), jnp.float32))

    def filter_tap(lag_index, running):
        lag_index = lag_index.astype(jnp.int32)
        window = lax.dynamic_slice_in_dim(padded_front, rim_rows - lag_index, TOKENS, 0)
        column = jnp.sum(grad_filtered * window * (capped >= lag_index)[:, None], axis=0)
        return lax.dynamic_update_slice_in_dim(running, column[:, None], lag_index, 1)

    grad_filters = lax.fori_loop(0, TAPS, filter_tap, jnp.zeros((CHANNELS, TAPS), jnp.float32)) * grad_scale
    grad_keys = (grad_product * values_wide).astype(jnp.bfloat16)
    grad_values = (grad_product * keys_wide).astype(jnp.bfloat16)
    return (grad_queries, grad_keys, grad_values, grad_filters, grad_weight)
```

```python
import functools

import jax
import jax.numpy as jnp
from jax import lax
from jax.experimental import pallas as pl
from jax.experimental.pallas import tpu as pltpu
from jax.sharding import PartitionSpec as P

MESH = pl.DeviceIdType.MESH
F32 = jnp.float32
BF16 = jnp.bfloat16
LANES = 128
GROUP = 64
WIDTH = 8


def kernel(
    ctx_n, tp_n,
    q_ref, k_ref, v_ref, f_ref, off_ref, w_hbm, og_ref,
    gq_ref, gk_ref, gv_ref, gf_ref, gw_ref,
    wbuf, gbuf, mixed, gm, filt, ext, gext, ft, capb, remb,
    psend, precv, hsend, hrecv, pbuf, xsend, xrecv, xown, rsend, rrecv,
    fg, frecv, fsum,
    w_sem, gs_sem, gr_sem, ps_sem, pr_sem, hs_sem, hr_sem,
    xs_sem, xr_sem, rs_sem, rr_sem, fs_sem, fr_sem, as_sem, ar_sem,
):
    i = lax.axis_index("ctx")
    r = lax.axis_index("tp")
    slab, chans = q_ref.shape
    taps = f_ref.shape[1]
    rows, features = og_ref.shape
    m = ctx_n // 2
    chunk = features // m
    oblk = features // ctx_n
    halves = chans // LANES
    share = taps // ctx_n
    core = lax.rem(i, 2)
    chip = lax.div(i, 2)
    sibling = i + 1 - 2 * core

    barrier = pltpu.get_barrier_semaphore()

    def greet(p, c):
        pl.semaphore_signal(barrier, inc=1, device_id={"ctx": lax.rem(i + p, ctx_n), "tp": r}, device_id_type=MESH)
        return c

    lax.fori_loop(1, ctx_n, greet, 0)

    @pl.when(r > 0)
    def _():
        pl.semaphore_signal(barrier, inc=1, device_id={"ctx": i, "tp": r - 1}, device_id_type=MESH)

    @pl.when(r < tp_n - 1)
    def _():
        pl.semaphore_signal(barrier, inc=1, device_id={"ctx": i, "tp": r + 1}, device_id_type=MESH)

    w_copy = pltpu.make_async_copy(w_hbm, wbuf, w_sem)
    w_copy.start()

    def target(step):
        off = m - 1 - step
        high = lax.rem(lax.div(chip, 2) + lax.div(off, 2), m // 2)
        low = lax.rem(lax.rem(chip, 2) + lax.rem(off, 2), 2)
        return 2 * high + low

    own_rows = pl.ds(pl.multiple_of(r * rows, 16), rows)

    def place(step, c):
        col = pl.multiple_of(target(step) * chunk, 128)
        gbuf[step, own_rows, :] = og_ref[:, pl.ds(col, chunk)]
        return c

    lax.fori_loop(0, m, place, 0)

    product = (k_ref[...].astype(F32) * v_ref[...].astype(F32)).astype(BF16)
    psend[...] = product[slab - taps:, :]
    for h in range(halves):
        ext[h, taps:, :] = product[:, h * LANES:(h + 1) * LANES].astype(F32)
    for h in range(halves):
        ft[h] = f_ref[h * LANES:(h + 1) * LANES, :].T

    lane_tok = lax.broadcasted_iota(jnp.int32, (slab, slab), 1)
    row_tok = lax.broadcasted_iota(jnp.int32, (slab, slab), 0)
    offs = jnp.broadcast_to(off_ref[...], (slab, slab))
    off_col = jnp.sum(jnp.where(lane_tok == row_tok, offs, 0).astype(F32), axis=1, keepdims=True)
    later = jnp.where((lane_tok > row_tok) & (offs == 0), lane_tok - row_tok - 1, taps - 1)
    rem_col = jnp.min(later.astype(F32), axis=1, keepdims=True)
    capb[...] = jnp.broadcast_to(off_col, (slab, LANES)).astype(jnp.int32)
    remb[...] = jnp.broadcast_to(jnp.minimum(rem_col, taps - 1), (slab, LANES)).astype(jnp.int32)
    gm[...] = jnp.zeros_like(gm)

    nbrs = jnp.where(r > 0, 1, 0) + jnp.where(r < tp_n - 1, 1, 0)
    pl.semaphore_wait(barrier, ctx_n - 1 + nbrs)

    def gather_copy(side, step, dist, source, dest):
        window = gbuf.at[step, pl.ds(pl.multiple_of(source * rows, 16), rows), :]
        return pltpu.make_async_remote_copy(
            src_ref=window, dst_ref=window,
            send_sem=gs_sem.at[side, step, dist], recv_sem=gr_sem.at[side, step, dist],
            device_id={"ctx": i, "tp": dest}, device_id_type=MESH,
        )

    def sends(side, step, dist, act):
        if side == 0:
            cond = (r - dist >= 0) & (r + 1 < tp_n)
            source, dest = r - dist, r + 1
        else:
            cond = (r + dist < tp_n) & (r >= 1)
            source, dest = r + dist, r - 1

        @pl.when(cond)
        def _():
            act(gather_copy(side, step, dist, source, dest))

    def arrives(side, step, dist):
        if side == 0:
            cond, source = r - 1 - dist >= 0, r - 1 - dist
            dest = r - 1
        else:
            cond, source = r + 1 + dist < tp_n, r + 1 + dist
            dest = r + 1

        @pl.when(cond)
        def _():
            gather_copy(side, step, dist, source, dest).wait_recv()

    def start(c):
        c.start()

    def done(c):
        c.wait_send()

    for step in range(min(2, m)):
        for side in range(2):
            sends(side, step, 0, start)

    p_copy = pltpu.make_async_remote_copy(
        src_ref=psend, dst_ref=precv, send_sem=ps_sem, recv_sem=pr_sem,
        device_id={"ctx": lax.rem(i + 1, ctx_n), "tp": r}, device_id_type=MESH,
    )
    p_copy.start()
    p_copy.wait()
    earlier = jnp.where(i > 0, precv[...].astype(F32), 0.0)
    for h in range(halves):
        ext[h, :taps, :] = earlier[:, h * LANES:(h + 1) * LANES]

    def tap_sum(source, base_row, sign, caps, emit):
        for g in range(slab // GROUP):
            t0 = g * GROUP
            cap = caps[t0:t0 + GROUP, :]

            def block(b, acc):
                acc = list(acc)
                for s in range(WIDTH):
                    j = b * WIDTH + s
                    keep = cap >= j
                    for h in range(halves):
                        window = source[h, pl.ds(base_row + t0 + sign * j, GROUP), :]
                        coeff = ft[h, pl.ds(j, 1), :]
                        acc[h] = acc[h] + jnp.where(keep, window * coeff, 0.0)
                return tuple(acc)

            zero = tuple(jnp.zeros((GROUP, LANES), F32) for _ in range(halves))
            acc = lax.fori_loop(0, taps // WIDTH, block, zero)
            for h in range(halves):
                emit(t0, h, acc[h])

    def emit_forward(t0, h, value):
        span, cols = slice(t0, t0 + GROUP), slice(h * LANES, (h + 1) * LANES)
        filt[span, cols] = value
        mixed[span, cols] = (q_ref[span, cols].astype(F32) * value).astype(BF16)

    tap_sum(ext, taps, -1, capb, emit_forward)
    w_copy.wait()

    def x_copy(step):
        return pltpu.make_async_remote_copy(
            src_ref=xsend.at[step], dst_ref=xrecv.at[step],
            send_sem=xs_sem.at[step], recv_sem=xr_sem.at[step],
            device_id={"ctx": sibling, "tp": r}, device_id_type=MESH,
        )

    def r_copy(step):
        return pltpu.make_async_remote_copy(
            src_ref=rsend.at[step], dst_ref=rrecv.at[step],
            send_sem=rs_sem.at[step], recv_sem=rr_sem.at[step],
            device_id={"ctx": 2 * target(step) + core, "tp": r}, device_id_type=MESH,
        )

    def forward_pair(step):
        x_copy(step).wait_recv()
        rsend[step] = (xown[step] + xrecv[step].astype(F32)).astype(BF16)
        r_copy(step).start()

    def main(step, c):
        @pl.when(step + 2 < m)
        def _():
            for side in range(2):
                sends(side, step + 2, 0, start)

        for dist in range(tp_n - 1):
            for side in range(2):
                arrives(side, step, dist)
                if dist + 1 < tp_n - 1:
                    sends(side, step, dist + 1, start)
        block = gbuf[step]
        pbuf[...] = lax.dot_general(block, mixed[...], (((0,), (0,)), ((), ())), preferred_element_type=F32)
        xsend[step] = pbuf[pl.ds(pl.multiple_of((1 - core) * oblk, 16), oblk), :].astype(BF16)
        x_copy(step).start()
        xown[step] = pbuf[pl.ds(pl.multiple_of(core * oblk, 16), oblk), :]
        span = pl.ds(pl.multiple_of(target(step) * chunk, 128), chunk)
        gm[...] += jnp.dot(block, wbuf[span, :], preferred_element_type=F32)

        @pl.when(step > 0)
        def _():
            forward_pair(step - 1)

        return c

    lax.fori_loop(0, m, main, 0)

    q_wide = q_ref[...].astype(F32)
    grad_mixed = gm[...]
    grad_filtered = (grad_mixed * q_wide).astype(BF16)
    wide = grad_filtered.astype(F32)
    lead_tok = lax.broadcasted_iota(jnp.int32, (taps, LANES), 0)
    for h in range(halves):
        part = wide[:, h * LANES:(h + 1) * LANES]
        gext[h, :slab, :] = part
        lead = jnp.where(capb[:taps, :] > lead_tok, part[:taps], 0.0)
        hsend[:, h * LANES:(h + 1) * LANES] = lead.astype(BF16)
    h_copy = pltpu.make_async_remote_copy(
        src_ref=hsend, dst_ref=hrecv, send_sem=hs_sem, recv_sem=hr_sem,
        device_id={"ctx": lax.rem(i + ctx_n - 1, ctx_n), "tp": r}, device_id_type=MESH,
    )
    h_copy.start()
    gq_ref[...] = (grad_mixed * filt[...]).astype(BF16)

    def tap_columns(b, c):
        for s in range(WIDTH):
            j = b * WIDTH + s
            total = [jnp.zeros((8, LANES), F32) for _ in range(halves)]
            for g in range(slab // GROUP):
                t0 = g * GROUP
                keep = capb[t0:t0 + GROUP, :] >= j
                for h in range(halves):
                    window = ext[h, pl.ds(taps + t0 - j, GROUP), :]
                    term = jnp.where(keep, window * gext[h, t0:t0 + GROUP, :], 0.0)
                    total[h] = total[h] + jnp.sum(term.reshape(GROUP // 8, 8, LANES), axis=0)
            for h in range(halves):
                fg[lax.div(j, share), h, pl.ds(lax.rem(j, share), 1), :] = jnp.sum(total[h], axis=0, keepdims=True)
        return c

    lax.fori_loop(0, taps // WIDTH, tap_columns, 0)

    def f_copy(p):
        peer = lax.rem(i + p, ctx_n)
        return pltpu.make_async_remote_copy(
            src_ref=fg.at[peer], dst_ref=frecv.at[p], send_sem=fs_sem.at[p], recv_sem=fr_sem.at[p],
            device_id={"ctx": peer, "tp": r}, device_id_type=MESH,
        )

    def a_copy(p):
        return pltpu.make_async_remote_copy(
            src_ref=fsum, dst_ref=gf_ref.at[i], send_sem=as_sem.at[p], recv_sem=ar_sem.at[p],
            device_id={"ctx": lax.rem(i + p, ctx_n), "tp": r}, device_id_type=MESH,
        )

    def a_arrival(p):
        source = lax.rem(i + ctx_n - p, ctx_n)
        return pltpu.make_async_remote_copy(
            src_ref=fsum, dst_ref=gf_ref.at[source], send_sem=as_sem.at[p], recv_sem=ar_sem.at[p],
            device_id={"ctx": source, "tp": r}, device_id_type=MESH,
        )

    def over_peers(act):
        def one(p, c):
            act(p)
            return c

        lax.fori_loop(1, ctx_n, one, 0)

    over_peers(lambda p: f_copy(p).start())

    h_copy.wait()
    follow = jnp.where(i < ctx_n - 1, hrecv[...].astype(F32), 0.0)
    for h in range(halves):
        gext[h, slab:, :] = follow[:, h * LANES:(h + 1) * LANES]

    def emit_backward(t0, h, value):
        span, cols = slice(t0, t0 + GROUP), slice(h * LANES, (h + 1) * LANES)
        gk_ref[span, cols] = (value * v_ref[span, cols].astype(F32)).astype(BF16)
        gv_ref[span, cols] = (value * k_ref[span, cols].astype(F32)).astype(BF16)

    over_peers(lambda p: f_copy(p).wait())
    frecv[0] = fg[i]
    fsum[...] = jnp.sum(frecv[...], axis=0)
    gf_ref[i] = fsum[...]
    over_peers(lambda p: a_copy(p).start())

    tap_sum(gext, 0, 1, remb, emit_backward)

    last = m - 1
    x_copy(last).wait_recv()
    gw_ref[...] = xown[last] + xrecv[last].astype(F32)

    def gather_sum(step, c):
        r_copy(step).wait_recv()
        gw_ref[...] += rrecv[step].astype(F32)
        return c

    lax.fori_loop(0, m - 1, gather_sum, 0)

    def drain(step, c):
        x_copy(step).wait_send()
        for dist in range(tp_n - 1):
            for side in range(2):
                sends(side, step, dist, done)

        @pl.when(step < m - 1)
        def _():
            r_copy(step).wait_send()

        return c

    lax.fori_loop(0, m, drain, 0)
    over_peers(lambda p: a_copy(p).wait_send())
    over_peers(lambda p: a_arrival(p).wait_recv())


def body(ctx_n, tp_n, queries, key_proj, value_proj, filters, offsets, out_weight, out_grads):
    slab, chans = queries.shape
    taps = filters.shape[1]
    rows, features = out_grads.shape
    m = ctx_n // 2
    chunk = features // m
    oblk = features // ctx_n
    halves = chans // LANES
    share = taps // ctx_n
    grad_scale = float(ctx_n * slab) ** (-0.5)
    dma = pltpu.SemaphoreType.DMA
    vmem = pl.BlockSpec(memory_space=pltpu.VMEM)
    sds = jax.ShapeDtypeStruct
    gq, gk, gv, gf, gw = pl.pallas_call(
        functools.partial(kernel, ctx_n, tp_n),
        out_shape=(
            sds((slab, chans), BF16), sds((slab, chans), BF16), sds((slab, chans), BF16),
            sds((ctx_n, halves, share, LANES), F32), sds((oblk, chans), F32),
        ),
        in_specs=[vmem] * 5 + [pl.BlockSpec(memory_space=pl.ANY), vmem],
        out_specs=(vmem,) * 5,
        scratch_shapes=[
            pltpu.VMEM((features, chans), BF16),
            pltpu.VMEM((m, slab, chunk), BF16),
            pltpu.VMEM((slab, chans), BF16),
            pltpu.VMEM((slab, chans), F32),
            pltpu.VMEM((slab, chans), F32),
            pltpu.VMEM((halves, slab + taps, LANES), F32),
            pltpu.VMEM((halves, slab + taps, LANES), F32),
            pltpu.VMEM((halves, taps, LANES), F32),
            pltpu.VMEM((slab, LANES), jnp.int32),
            pltpu.VMEM((slab, LANES), jnp.int32),
            pltpu.VMEM((taps, chans), BF16),
            pltpu.VMEM((taps, chans), BF16),
            pltpu.VMEM((taps, chans), BF16),
            pltpu.VMEM((taps, chans), BF16),
            pltpu.VMEM((chunk, chans), F32),
            pltpu.VMEM((m, oblk, chans), BF16),
            pltpu.VMEM((m, oblk, chans), BF16),
            pltpu.VMEM((m, oblk, chans), F32),
            pltpu.VMEM((m, oblk, chans), BF16),
            pltpu.VMEM((m, oblk, chans), BF16),
            pltpu.VMEM((ctx_n, halves, share, LANES), F32),
            pltpu.VMEM((ctx_n, halves, share, LANES), F32),
            pltpu.VMEM((halves, share, LANES), F32),
            dma, dma((2, m, tp_n)), dma((2, m, tp_n)), dma, dma, dma, dma,
            dma((m,)), dma((m,)), dma((m,)), dma((m,)),
            dma((ctx_n,)), dma((ctx_n,)), dma((ctx_n,)), dma((ctx_n,)),
        ],
        compiler_params=pltpu.CompilerParams(
            collective_id=0, has_side_effects=True, vmem_limit_bytes=48 * 1024 * 1024
        ),
    )(queries, key_proj, value_proj, filters, offsets.reshape(1, slab), out_weight, out_grads)
    grad_filters = jnp.transpose(gf * grad_scale, (1, 3, 0, 2)).reshape(chans, taps)
    return gq, gk, gv, grad_filters, gw * grad_scale


def solution(mesh):
    in_specs = (
        P("ctx", "tp"),
        P("ctx", "tp"),
        P("ctx", "tp"),
        P("tp", None),
        P("ctx"),
        P(None, "tp"),
        P(("ctx", "tp"), None),
    )
    out_specs = (P("ctx", "tp"), P("ctx", "tp"), P("ctx", "tp"), P("tp", None), P("ctx", "tp"))
    step = functools.partial(body, mesh.shape["ctx"], mesh.shape["tp"])
    return jax.shard_map(step, mesh=mesh, in_specs=in_specs, out_specs=out_specs, check_vma=False)
```

```python
import functools

import jax
import jax.numpy as jnp
from jax import lax
from jax.experimental import pallas as pl
from jax.experimental.pallas import tpu as pltpu
from jax.sharding import PartitionSpec as P

MESH = pl.DeviceIdType.MESH
F32 = jnp.float32
BF16 = jnp.bfloat16
LANES = 128
GROUP = 64
WIDTH = 8


def kernel(
    ctx_n, tp_n,
    q_hbm, k_hbm, v_hbm, f_hbm, off_hbm, w_hbm, og_ref,
    gq_ref, gk_ref, gv_ref, gf_ref, gw_ref,
    wbuf, gbuf, mixed, gm, filt, ext, gext, ft, capb, remb,
    psend, precv, hsend, hrecv, pbuf, xsend, xrecv, xown, rsend, rrecv,
    fg, frecv, fsum, q_ref, k_ref, v_ref, f_ref, off_ref,
    in_sem, og_sem, w_sem, gs_sem, gr_sem, ps_sem, pr_sem, hs_sem, hr_sem,
    xs_sem, xr_sem, rs_sem, rr_sem, fs_sem, fr_sem, as_sem, ar_sem,
):
    i = lax.axis_index("ctx")
    r = lax.axis_index("tp")
    slab, chans = q_ref.shape
    taps = f_ref.shape[1]
    rows, features = og_ref.shape
    m = ctx_n // 2
    chunk = features // m
    oblk = features // ctx_n
    halves = chans // LANES
    share = taps // ctx_n
    core = lax.rem(i, 2)
    chip = lax.div(i, 2)
    sibling = i + 1 - 2 * core

    barrier = pltpu.get_barrier_semaphore()

    def greet(p, c):
        pl.semaphore_signal(barrier, inc=1, device_id={"ctx": lax.rem(i + p, ctx_n), "tp": r}, device_id_type=MESH)
        return c

    lax.fori_loop(1, ctx_n, greet, 0)

    @pl.when(r > 0)
    def _():
        pl.semaphore_signal(barrier, inc=1, device_id={"ctx": i, "tp": r - 1}, device_id_type=MESH)

    @pl.when(r < tp_n - 1)
    def _():
        pl.semaphore_signal(barrier, inc=1, device_id={"ctx": i, "tp": r + 1}, device_id_type=MESH)

    def target(step):
        off = m - 1 - step
        high = lax.rem(lax.div(chip, 2) + lax.div(off, 2), m // 2)
        low = lax.rem(lax.rem(chip, 2) + lax.rem(off, 2), 2)
        return 2 * high + low

    own_rows = pl.ds(pl.multiple_of(r * rows, 16), rows)

    def own_columns(step):
        return og_ref.at[:, pl.ds(pl.multiple_of(target(step) * chunk, 128), chunk)]

    def place(step):
        return pltpu.make_async_copy(own_columns(step), gbuf.at[step, own_rows, :], og_sem.at[step])

    loads = [
        pltpu.make_async_copy(source, held, in_sem.at[n])
        for n, (source, held) in enumerate((
            (k_hbm, k_ref), (v_hbm, v_ref), (off_hbm, off_ref), (f_hbm, f_ref), (q_hbm, q_ref)
        ))
    ]
    for load in loads:
        load.start()

    def place_all(step, c):
        place(step).start()
        return c

    lax.fori_loop(0, m, place_all, 0)
    w_copy = pltpu.make_async_copy(w_hbm, wbuf, w_sem)
    w_copy.start()
    nbrs = jnp.where(r > 0, 1, 0) + jnp.where(r < tp_n - 1, 1, 0)
    pl.semaphore_wait(barrier, ctx_n - 1 + nbrs)

    def gather_copy(side, step, dist, source, dest):
        window = gbuf.at[step, pl.ds(pl.multiple_of(source * rows, 16), rows), :]
        return pltpu.make_async_remote_copy(
            src_ref=own_columns(step) if dist == 0 else window, dst_ref=window,
            send_sem=gs_sem.at[side, step, dist], recv_sem=gr_sem.at[side, step, dist],
            device_id={"ctx": i, "tp": dest}, device_id_type=MESH,
        )

    def sends(side, step, dist, act):
        if side == 0:
            cond = (r - dist >= 0) & (r + 1 < tp_n)
            source, dest = r - dist, r + 1
        else:
            cond = (r + dist < tp_n) & (r >= 1)
            source, dest = r + dist, r - 1

        @pl.when(cond)
        def _():
            act(gather_copy(side, step, dist, source, dest))

    def arrives(side, step, dist):
        if side == 0:
            cond, source = r - 1 - dist >= 0, r - 1 - dist
            dest = r - 1
        else:
            cond, source = r + 1 + dist < tp_n, r + 1 + dist
            dest = r + 1

        @pl.when(cond)
        def _():
            gather_copy(side, step, dist, source, dest).wait_recv()

    def start(c):
        c.start()

    def done(c):
        c.wait_send()

    for step in range(min(2, m)):
        for side in range(2):
            sends(side, step, 0, start)


    loads[0].wait()
    loads[1].wait()
    product = (k_ref[...].astype(F32) * v_ref[...].astype(F32)).astype(BF16)
    psend[...] = product[slab - taps:, :]
    p_copy = pltpu.make_async_remote_copy(
        src_ref=psend, dst_ref=precv, send_sem=ps_sem, recv_sem=pr_sem,
        device_id={"ctx": lax.rem(i + 1, ctx_n), "tp": r}, device_id_type=MESH,
    )
    p_copy.start()
    for h in range(halves):
        ext[h, taps:, :] = product[:, h * LANES:(h + 1) * LANES].astype(F32)
    loads[2].wait()
    loads[3].wait()
    for h in range(halves):
        ft[h] = f_ref[h * LANES:(h + 1) * LANES, :].T

    lane_tok = lax.broadcasted_iota(jnp.int32, (slab, slab), 1)
    row_tok = lax.broadcasted_iota(jnp.int32, (slab, slab), 0)
    offs = jnp.broadcast_to(off_ref[...], (slab, slab))
    off_col = jnp.sum(jnp.where(lane_tok == row_tok, offs, 0).astype(F32), axis=1, keepdims=True)
    later = jnp.where((lane_tok > row_tok) & (offs == 0), lane_tok - row_tok - 1, taps - 1)
    rem_col = jnp.min(later.astype(F32), axis=1, keepdims=True)
    capb[...] = jnp.broadcast_to(off_col, (slab, LANES)).astype(jnp.int32)
    remb[...] = jnp.broadcast_to(jnp.minimum(rem_col, taps - 1), (slab, LANES)).astype(jnp.int32)
    gm[...] = jnp.zeros_like(gm)

    loads[4].wait()
    p_copy.wait()
    earlier = jnp.where(i > 0, precv[...].astype(F32), 0.0)
    for h in range(halves):
        ext[h, :taps, :] = earlier[:, h * LANES:(h + 1) * LANES]

    def tap_sum(source, base_row, sign, caps, emit):
        for g in range(slab // GROUP):
            t0 = g * GROUP
            cap = caps[t0:t0 + GROUP, :]

            def block(b, acc):
                acc = list(acc)
                for s in range(WIDTH):
                    j = b * WIDTH + s
                    keep = cap >= j
                    for h in range(halves):
                        window = source[h, pl.ds(base_row + t0 + sign * j, GROUP), :]
                        coeff = ft[h, pl.ds(j, 1), :]
                        acc[h] = acc[h] + jnp.where(keep, window * coeff, 0.0)
                return tuple(acc)

            zero = tuple(jnp.zeros((GROUP, LANES), F32) for _ in range(halves))
            acc = lax.fori_loop(0, taps // WIDTH, block, zero)
            for h in range(halves):
                emit(t0, h, acc[h])

    def emit_forward(t0, h, value):
        span, cols = slice(t0, t0 + GROUP), slice(h * LANES, (h + 1) * LANES)
        filt[span, cols] = value
        mixed[span, cols] = (q_ref[span, cols].astype(F32) * value).astype(BF16)

    tap_sum(ext, taps, -1, capb, emit_forward)
    w_copy.wait()

    def x_copy(step):
        return pltpu.make_async_remote_copy(
            src_ref=xsend.at[step], dst_ref=xrecv.at[step],
            send_sem=xs_sem.at[step], recv_sem=xr_sem.at[step],
            device_id={"ctx": sibling, "tp": r}, device_id_type=MESH,
        )

    def r_copy(step):
        return pltpu.make_async_remote_copy(
            src_ref=rsend.at[step], dst_ref=rrecv.at[step],
            send_sem=rs_sem.at[step], recv_sem=rr_sem.at[step],
            device_id={"ctx": 2 * target(step) + core, "tp": r}, device_id_type=MESH,
        )

    def forward_pair(step):
        x_copy(step).wait_recv()
        rsend[step] = (xown[step] + xrecv[step].astype(F32)).astype(BF16)
        r_copy(step).start()

    def main(step, c):
        @pl.when(step + 2 < m)
        def _():
            for side in range(2):
                sends(side, step + 2, 0, start)

        place(step).wait()
        for dist in range(tp_n - 1):
            for side in range(2):
                arrives(side, step, dist)
                if dist + 1 < tp_n - 1:
                    sends(side, step, dist + 1, start)
            if dist == 0:

                @pl.when(step > 0)
                def _():
                    forward_pair(step - 1)

        block = gbuf[step]
        pbuf[...] = lax.dot_general(block, mixed[...], (((0,), (0,)), ((), ())), preferred_element_type=F32)
        xsend[step] = pbuf[pl.ds(pl.multiple_of((1 - core) * oblk, 16), oblk), :].astype(BF16)
        x_copy(step).start()
        xown[step] = pbuf[pl.ds(pl.multiple_of(core * oblk, 16), oblk), :]
        span = pl.ds(pl.multiple_of(target(step) * chunk, 128), chunk)
        gm[...] += jnp.dot(block, wbuf[span, :], preferred_element_type=F32)

        return c

    lax.fori_loop(0, m, main, 0)

    q_wide = q_ref[...].astype(F32)
    grad_mixed = gm[...]
    grad_filtered = (grad_mixed * q_wide).astype(BF16)
    wide = grad_filtered.astype(F32)
    lead_tok = lax.broadcasted_iota(jnp.int32, (taps, LANES), 0)
    for h in range(halves):
        part = wide[:, h * LANES:(h + 1) * LANES]
        gext[h, :slab, :] = part
        lead = jnp.where(capb[:taps, :] > lead_tok, part[:taps], 0.0)
        hsend[:, h * LANES:(h + 1) * LANES] = lead.astype(BF16)
    h_copy = pltpu.make_async_remote_copy(
        src_ref=hsend, dst_ref=hrecv, send_sem=hs_sem, recv_sem=hr_sem,
        device_id={"ctx": lax.rem(i + ctx_n - 1, ctx_n), "tp": r}, device_id_type=MESH,
    )
    h_copy.start()
    gq_ref[...] = (grad_mixed * filt[...]).astype(BF16)

    def tap_columns(b, c):
        for s in range(WIDTH):
            j = b * WIDTH + s
            total = [jnp.zeros((8, LANES), F32) for _ in range(halves)]
            for g in range(slab // GROUP):
                t0 = g * GROUP
                keep = capb[t0:t0 + GROUP, :] >= j
                for h in range(halves):
                    window = ext[h, pl.ds(taps + t0 - j, GROUP), :]
                    term = jnp.where(keep, window * gext[h, t0:t0 + GROUP, :], 0.0)
                    total[h] = total[h] + jnp.sum(term.reshape(GROUP // 8, 8, LANES), axis=0)
            for h in range(halves):
                fg[lax.div(j, share), h, pl.ds(lax.rem(j, share), 1), :] = jnp.sum(total[h], axis=0, keepdims=True)
        return c

    lax.fori_loop(0, taps // WIDTH, tap_columns, 0)

    def f_copy(p):
        peer = lax.rem(i + p, ctx_n)
        return pltpu.make_async_remote_copy(
            src_ref=fg.at[peer], dst_ref=frecv.at[p], send_sem=fs_sem.at[p], recv_sem=fr_sem.at[p],
            device_id={"ctx": peer, "tp": r}, device_id_type=MESH,
        )

    def a_copy(p):
        return pltpu.make_async_remote_copy(
            src_ref=fsum, dst_ref=gf_ref.at[i], send_sem=as_sem.at[p], recv_sem=ar_sem.at[p],
            device_id={"ctx": lax.rem(i + p, ctx_n), "tp": r}, device_id_type=MESH,
        )

    def a_arrival(p):
        source = lax.rem(i + ctx_n - p, ctx_n)
        return pltpu.make_async_remote_copy(
            src_ref=fsum, dst_ref=gf_ref.at[source], send_sem=as_sem.at[p], recv_sem=ar_sem.at[p],
            device_id={"ctx": source, "tp": r}, device_id_type=MESH,
        )

    def over_peers(act):
        def one(p, c):
            act(p)
            return c

        lax.fori_loop(1, ctx_n, one, 0)

    over_peers(lambda p: f_copy(p).start())

    h_copy.wait()
    follow = jnp.where(i < ctx_n - 1, hrecv[...].astype(F32), 0.0)
    for h in range(halves):
        gext[h, slab:, :] = follow[:, h * LANES:(h + 1) * LANES]

    def emit_backward(t0, h, value):
        span, cols = slice(t0, t0 + GROUP), slice(h * LANES, (h + 1) * LANES)
        gk_ref[span, cols] = (value * v_ref[span, cols].astype(F32)).astype(BF16)
        gv_ref[span, cols] = (value * k_ref[span, cols].astype(F32)).astype(BF16)

    over_peers(lambda p: f_copy(p).wait())
    frecv[0] = fg[i]
    fsum[...] = jnp.sum(frecv[...], axis=0)
    gf_ref[i] = fsum[...]
    over_peers(lambda p: a_copy(p).start())

    tap_sum(gext, 0, 1, remb, emit_backward)

    last = m - 1
    x_copy(last).wait_recv()
    gw_ref[...] = xown[last] + xrecv[last].astype(F32)

    def gather_sum(step, c):
        r_copy(step).wait_recv()
        gw_ref[...] += rrecv[step].astype(F32)
        return c

    lax.fori_loop(0, m - 1, gather_sum, 0)

    def drain(step, c):
        x_copy(step).wait_send()
        for dist in range(tp_n - 1):
            for side in range(2):
                sends(side, step, dist, done)

        @pl.when(step < m - 1)
        def _():
            r_copy(step).wait_send()

        return c

    lax.fori_loop(0, m, drain, 0)
    over_peers(lambda p: a_copy(p).wait_send())
    over_peers(lambda p: a_arrival(p).wait_recv())


def finish(scale, gq_ref, gk_ref, gv_ref, gf_ref, gw_ref, oq_ref, ok_ref, ov_ref, of_ref, ow_ref, flat):
    ow_ref[...] = gw_ref[...] * scale
    oq_ref[...] = gq_ref[...]
    ok_ref[...] = gk_ref[...]
    ov_ref[...] = gv_ref[...]
    parts, halves, share, lanes = gf_ref.shape
    for h in range(halves):
        for part in range(parts):
            flat[part * share:(part + 1) * share, :] = gf_ref[part, h] * scale
        of_ref[h * lanes:(h + 1) * lanes, :] = flat[...].T


def body(ctx_n, tp_n, queries, key_proj, value_proj, filters, offsets, out_weight, out_grads):
    slab, chans = queries.shape
    taps = filters.shape[1]
    rows, features = out_grads.shape
    m = ctx_n // 2
    chunk = features // m
    oblk = features // ctx_n
    halves = chans // LANES
    share = taps // ctx_n
    grad_scale = float(ctx_n * slab) ** (-0.5)
    dma = pltpu.SemaphoreType.DMA
    vmem = pl.BlockSpec(memory_space=pltpu.VMEM)
    sds = jax.ShapeDtypeStruct
    gq, gk, gv, gf, gw = pl.pallas_call(
        functools.partial(kernel, ctx_n, tp_n),
        out_shape=(
            sds((slab, chans), BF16), sds((slab, chans), BF16), sds((slab, chans), BF16),
            sds((ctx_n, halves, share, LANES), F32), sds((oblk, chans), F32),
        ),
        in_specs=[pl.BlockSpec(memory_space=pl.ANY)] * 7,
        out_specs=(vmem,) * 5,
        scratch_shapes=[
            pltpu.VMEM((features, chans), BF16),
            pltpu.VMEM((m, slab, chunk), BF16),
            pltpu.VMEM((slab, chans), BF16),
            pltpu.VMEM((slab, chans), F32),
            pltpu.VMEM((slab, chans), F32),
            pltpu.VMEM((halves, slab + taps, LANES), F32),
            pltpu.VMEM((halves, slab + taps, LANES), F32),
            pltpu.VMEM((halves, taps, LANES), F32),
            pltpu.VMEM((slab, LANES), jnp.int32),
            pltpu.VMEM((slab, LANES), jnp.int32),
            pltpu.VMEM((taps, chans), BF16),
            pltpu.VMEM((taps, chans), BF16),
            pltpu.VMEM((taps, chans), BF16),
            pltpu.VMEM((taps, chans), BF16),
            pltpu.VMEM((chunk, chans), F32),
            pltpu.VMEM((m, oblk, chans), BF16),
            pltpu.VMEM((m, oblk, chans), BF16),
            pltpu.VMEM((m, oblk, chans), F32),
            pltpu.VMEM((m, oblk, chans), BF16),
            pltpu.VMEM((m, oblk, chans), BF16),
            pltpu.VMEM((ctx_n, halves, share, LANES), F32),
            pltpu.VMEM((ctx_n, halves, share, LANES), F32),
            pltpu.VMEM((halves, share, LANES), F32),
            pltpu.VMEM((slab, chans), BF16),
            pltpu.VMEM((slab, chans), BF16),
            pltpu.VMEM((slab, chans), BF16),
            pltpu.VMEM((chans, taps), F32),
            pltpu.VMEM((1, slab), jnp.int32),
            dma((5,)), dma((m,)), dma, dma((2, m, tp_n)), dma((2, m, tp_n)), dma, dma, dma, dma,
            dma((m,)), dma((m,)), dma((m,)), dma((m,)),
            dma((ctx_n,)), dma((ctx_n,)), dma((ctx_n,)), dma((ctx_n,)),
        ],
        compiler_params=pltpu.CompilerParams(
            collective_id=0, has_side_effects=True, vmem_limit_bytes=62 * 1024 * 1024
        ),
    )(queries, key_proj, value_proj, filters, offsets.reshape(1, slab), out_weight, out_grads)
    return pl.pallas_call(
        functools.partial(finish, grad_scale),
        out_shape=(
            sds((slab, chans), BF16), sds((slab, chans), BF16), sds((slab, chans), BF16),
            sds((chans, taps), F32), sds((oblk, chans), F32),
        ),
        in_specs=[vmem] * 5,
        out_specs=(vmem,) * 5,
        scratch_shapes=[pltpu.VMEM((taps, LANES), F32)],
    )(gq, gk, gv, gf, gw)


def solution(mesh):
    in_specs = (
        P("ctx", "tp"),
        P("ctx", "tp"),
        P("ctx", "tp"),
        P("tp", None),
        P("ctx"),
        P(None, "tp"),
        P(("ctx", "tp"), None),
    )
    out_specs = (P("ctx", "tp"), P("ctx", "tp"), P("ctx", "tp"), P("tp", None), P("ctx", "tp"))
    step = functools.partial(body, mesh.shape["ctx"], mesh.shape["tp"])
    return jax.shard_map(step, mesh=mesh, in_specs=in_specs, out_specs=out_specs, check_vma=False)
```

```python
import functools

import jax
import jax.numpy as jnp
from jax import lax
from jax.experimental import pallas as pl
from jax.experimental.pallas import tpu as pltpu
from jax.sharding import PartitionSpec as P

MESH = pl.DeviceIdType.MESH
F32 = jnp.float32
BF16 = jnp.bfloat16
LANES = 128
GROUP = 64
WIDTH = 8


def kernel(
    ctx_n, tp_n,
    q_hbm, k_hbm, v_hbm, f_hbm, off_hbm, w_hbm, og_ref,
    gq_ref, gk_ref, gv_ref, gf_ref, gw_ref,
    wbuf, gbuf, mixed, gm, filt, ext, gext, ft, capb, remb,
    psend, precv, hsend, hrecv, pbuf, xsend, xrecv, xown, rsend, rrecv,
    fg, frecv, fsum, q_ref, k_ref, v_ref, f_ref, off_ref,
    in_sem, og_sem, w_sem, gs_sem, gr_sem, ps_sem, pr_sem, hs_sem, hr_sem,
    xs_sem, xr_sem, rs_sem, rr_sem, fs_sem, fr_sem, as_sem, ar_sem,
):
    i = lax.axis_index("ctx")
    r = lax.axis_index("tp")
    slab, chans = q_ref.shape
    taps = f_ref.shape[1]
    rows, features = og_ref.shape
    m = ctx_n // 2
    chunk = features // m
    oblk = features // ctx_n
    halves = chans // LANES
    share = taps // ctx_n
    core = lax.rem(i, 2)
    chip = lax.div(i, 2)
    sibling = i + 1 - 2 * core

    barrier = pltpu.get_barrier_semaphore()

    def greet(p, c):
        pl.semaphore_signal(barrier, inc=1, device_id={"ctx": lax.rem(i + p, ctx_n), "tp": r}, device_id_type=MESH)
        return c

    lax.fori_loop(1, ctx_n, greet, 0)

    @pl.when(r > 0)
    def _():
        pl.semaphore_signal(barrier, inc=1, device_id={"ctx": i, "tp": r - 1}, device_id_type=MESH)

    @pl.when(r < tp_n - 1)
    def _():
        pl.semaphore_signal(barrier, inc=1, device_id={"ctx": i, "tp": r + 1}, device_id_type=MESH)

    def target(step):
        off = m - 1 - step
        high = lax.rem(lax.div(chip, 2) + lax.div(off, 2), m // 2)
        low = lax.rem(lax.rem(chip, 2) + lax.rem(off, 2), 2)
        return 2 * high + low

    own_rows = pl.ds(pl.multiple_of(r * rows, 16), rows)

    def own_columns(step):
        return og_ref.at[:, pl.ds(pl.multiple_of(target(step) * chunk, 128), chunk)]

    def place(step):
        return pltpu.make_async_copy(own_columns(step), gbuf.at[step, own_rows, :], og_sem.at[step])

    loads = [
        pltpu.make_async_copy(source, held, in_sem.at[n])
        for n, (source, held) in enumerate((
            (k_hbm, k_ref), (v_hbm, v_ref), (off_hbm, off_ref), (f_hbm, f_ref), (q_hbm, q_ref)
        ))
    ]
    for load in loads:
        load.start()

    def place_all(step, c):
        place(step).start()
        return c

    lax.fori_loop(0, m, place_all, 0)
    w_copy = pltpu.make_async_copy(w_hbm, wbuf, w_sem)
    w_copy.start()
    nbrs = jnp.where(r > 0, 1, 0) + jnp.where(r < tp_n - 1, 1, 0)
    pl.semaphore_wait(barrier, ctx_n - 1 + nbrs)

    def gather_copy(side, step, dist, source, dest):
        window = gbuf.at[step, pl.ds(pl.multiple_of(source * rows, 16), rows), :]
        return pltpu.make_async_remote_copy(
            src_ref=own_columns(step) if dist == 0 else window, dst_ref=window,
            send_sem=gs_sem.at[side, step, dist], recv_sem=gr_sem.at[side, step, dist],
            device_id={"ctx": i, "tp": dest}, device_id_type=MESH,
        )

    def sends(side, step, dist, act):
        if side == 0:
            cond = (r - dist >= 0) & (r + 1 < tp_n)
            source, dest = r - dist, r + 1
        else:
            cond = (r + dist < tp_n) & (r >= 1)
            source, dest = r + dist, r - 1

        @pl.when(cond)
        def _():
            act(gather_copy(side, step, dist, source, dest))

    def arrives(side, step, dist):
        if side == 0:
            cond, source = r - 1 - dist >= 0, r - 1 - dist
            dest = r - 1
        else:
            cond, source = r + 1 + dist < tp_n, r + 1 + dist
            dest = r + 1

        @pl.when(cond)
        def _():
            gather_copy(side, step, dist, source, dest).wait_recv()

    def start(c):
        c.start()

    def done(c):
        c.wait_send()

    for step in range(min(4, m)):
        for side in range(2):
            sends(side, step, 0, start)


    loads[0].wait()
    loads[1].wait()
    product = (k_ref[...].astype(F32) * v_ref[...].astype(F32)).astype(BF16)
    psend[...] = product[slab - taps:, :]
    p_copy = pltpu.make_async_remote_copy(
        src_ref=psend, dst_ref=precv, send_sem=ps_sem, recv_sem=pr_sem,
        device_id={"ctx": lax.rem(i + 1, ctx_n), "tp": r}, device_id_type=MESH,
    )
    p_copy.start()
    for h in range(halves):
        ext[h, taps:, :] = product[:, h * LANES:(h + 1) * LANES].astype(F32)
    loads[2].wait()
    loads[3].wait()
    for h in range(halves):
        ft[h] = f_ref[h * LANES:(h + 1) * LANES, :].T

    lane_tok = lax.broadcasted_iota(jnp.int32, (slab, slab), 1)
    row_tok = lax.broadcasted_iota(jnp.int32, (slab, slab), 0)
    offs = jnp.broadcast_to(off_ref[...], (slab, slab))
    off_col = jnp.sum(jnp.where(lane_tok == row_tok, offs, 0).astype(F32), axis=1, keepdims=True)
    later = jnp.where((lane_tok > row_tok) & (offs == 0), lane_tok - row_tok - 1, taps - 1)
    rem_col = jnp.min(later.astype(F32), axis=1, keepdims=True)
    capb[...] = jnp.broadcast_to(off_col, (slab, LANES)).astype(jnp.int32)
    remb[...] = jnp.broadcast_to(jnp.minimum(rem_col, taps - 1), (slab, LANES)).astype(jnp.int32)
    gm[...] = jnp.zeros_like(gm)

    loads[4].wait()
    p_copy.wait()
    earlier = jnp.where(i > 0, precv[...].astype(F32), 0.0)
    for h in range(halves):
        ext[h, :taps, :] = earlier[:, h * LANES:(h + 1) * LANES]

    def tap_sum(source, base_row, sign, caps, emit):
        for g in range(slab // GROUP):
            t0 = g * GROUP
            cap = caps[t0:t0 + GROUP, :]

            def block(b, acc):
                acc = list(acc)
                for s in range(WIDTH):
                    j = b * WIDTH + s
                    keep = cap >= j
                    for h in range(halves):
                        window = source[h, pl.ds(base_row + t0 + sign * j, GROUP), :]
                        coeff = ft[h, pl.ds(j, 1), :]
                        acc[h] = acc[h] + jnp.where(keep, window * coeff, 0.0)
                return tuple(acc)

            zero = tuple(jnp.zeros((GROUP, LANES), F32) for _ in range(halves))
            acc = lax.fori_loop(0, taps // WIDTH, block, zero)
            for h in range(halves):
                emit(t0, h, acc[h])

    def emit_forward(t0, h, value):
        span, cols = slice(t0, t0 + GROUP), slice(h * LANES, (h + 1) * LANES)
        filt[span, cols] = value
        mixed[span, cols] = (q_ref[span, cols].astype(F32) * value).astype(BF16)

    tap_sum(ext, taps, -1, capb, emit_forward)
    w_copy.wait()

    def x_copy(step):
        return pltpu.make_async_remote_copy(
            src_ref=xsend.at[step], dst_ref=xrecv.at[step],
            send_sem=xs_sem.at[step], recv_sem=xr_sem.at[step],
            device_id={"ctx": sibling, "tp": r}, device_id_type=MESH,
        )

    def r_copy(step):
        return pltpu.make_async_remote_copy(
            src_ref=rsend.at[step], dst_ref=rrecv.at[step],
            send_sem=rs_sem.at[step], recv_sem=rr_sem.at[step],
            device_id={"ctx": 2 * target(step) + core, "tp": r}, device_id_type=MESH,
        )

    def forward_pair(step):
        x_copy(step).wait_recv()
        rsend[step] = (xown[step] + xrecv[step].astype(F32)).astype(BF16)
        r_copy(step).start()

    def main(step, c):
        @pl.when(step + 4 < m)
        def _():
            for side in range(2):
                sends(side, step + 4, 0, start)

        place(step).wait()
        for dist in range(tp_n - 1):
            for side in range(2):
                arrives(side, step, dist)
                if dist + 1 < tp_n - 1:
                    sends(side, step, dist + 1, start)
            if dist == 0:

                @pl.when(step > 0)
                def _():
                    forward_pair(step - 1)

        block = gbuf[step]
        pbuf[...] = lax.dot_general(block, mixed[...], (((0,), (0,)), ((), ())), preferred_element_type=F32)
        xsend[step] = pbuf[pl.ds(pl.multiple_of((1 - core) * oblk, 16), oblk), :].astype(BF16)
        x_copy(step).start()
        xown[step] = pbuf[pl.ds(pl.multiple_of(core * oblk, 16), oblk), :]
        span = pl.ds(pl.multiple_of(target(step) * chunk, 128), chunk)
        gm[...] += jnp.dot(block, wbuf[span, :], preferred_element_type=F32)

        return c

    lax.fori_loop(0, m, main, 0)

    q_wide = q_ref[...].astype(F32)
    grad_mixed = gm[...]
    grad_filtered = (grad_mixed * q_wide).astype(BF16)
    wide = grad_filtered.astype(F32)
    lead_tok = lax.broadcasted_iota(jnp.int32, (taps, LANES), 0)
    for h in range(halves):
        part = wide[:, h * LANES:(h + 1) * LANES]
        gext[h, :slab, :] = part
        lead = jnp.where(capb[:taps, :] > lead_tok, part[:taps], 0.0)
        hsend[:, h * LANES:(h + 1) * LANES] = lead.astype(BF16)
    h_copy = pltpu.make_async_remote_copy(
        src_ref=hsend, dst_ref=hrecv, send_sem=hs_sem, recv_sem=hr_sem,
        device_id={"ctx": lax.rem(i + ctx_n - 1, ctx_n), "tp": r}, device_id_type=MESH,
    )
    h_copy.start()
    gq_ref[...] = (grad_mixed * filt[...]).astype(BF16)

    def tap_columns(b, c):
        for s in range(WIDTH):
            j = b * WIDTH + s
            total = [jnp.zeros((8, LANES), F32) for _ in range(halves)]
            for g in range(slab // GROUP):
                t0 = g * GROUP
                keep = capb[t0:t0 + GROUP, :] >= j
                for h in range(halves):
                    window = ext[h, pl.ds(taps + t0 - j, GROUP), :]
                    term = jnp.where(keep, window * gext[h, t0:t0 + GROUP, :], 0.0)
                    total[h] = total[h] + jnp.sum(term.reshape(GROUP // 8, 8, LANES), axis=0)
            for h in range(halves):
                fg[lax.div(j, share), h, pl.ds(lax.rem(j, share), 1), :] = jnp.sum(total[h], axis=0, keepdims=True)
        return c

    lax.fori_loop(0, taps // WIDTH, tap_columns, 0)

    def f_copy(p):
        peer = lax.rem(i + p, ctx_n)
        return pltpu.make_async_remote_copy(
            src_ref=fg.at[peer], dst_ref=frecv.at[p], send_sem=fs_sem.at[p], recv_sem=fr_sem.at[p],
            device_id={"ctx": peer, "tp": r}, device_id_type=MESH,
        )

    def a_copy(p):
        return pltpu.make_async_remote_copy(
            src_ref=fsum, dst_ref=gf_ref.at[i], send_sem=as_sem.at[p], recv_sem=ar_sem.at[p],
            device_id={"ctx": lax.rem(i + p, ctx_n), "tp": r}, device_id_type=MESH,
        )

    def a_arrival(p):
        source = lax.rem(i + ctx_n - p, ctx_n)
        return pltpu.make_async_remote_copy(
            src_ref=fsum, dst_ref=gf_ref.at[source], send_sem=as_sem.at[p], recv_sem=ar_sem.at[p],
            device_id={"ctx": source, "tp": r}, device_id_type=MESH,
        )

    def over_peers(act):
        def one(p, c):
            act(p)
            return c

        lax.fori_loop(1, ctx_n, one, 0)

    over_peers(lambda p: f_copy(p).start())

    h_copy.wait()
    follow = jnp.where(i < ctx_n - 1, hrecv[...].astype(F32), 0.0)
    for h in range(halves):
        gext[h, slab:, :] = follow[:, h * LANES:(h + 1) * LANES]

    def emit_backward(t0, h, value):
        span, cols = slice(t0, t0 + GROUP), slice(h * LANES, (h + 1) * LANES)
        gk_ref[span, cols] = (value * v_ref[span, cols].astype(F32)).astype(BF16)
        gv_ref[span, cols] = (value * k_ref[span, cols].astype(F32)).astype(BF16)

    over_peers(lambda p: f_copy(p).wait())
    frecv[0] = fg[i]
    fsum[...] = jnp.sum(frecv[...], axis=0)
    gf_ref[i] = fsum[...]
    over_peers(lambda p: a_copy(p).start())

    tap_sum(gext, 0, 1, remb, emit_backward)

    last = m - 1
    x_copy(last).wait_recv()
    gw_ref[...] = xown[last] + xrecv[last].astype(F32)

    def gather_sum(step, c):
        r_copy(step).wait_recv()
        gw_ref[...] += rrecv[step].astype(F32)
        return c

    lax.fori_loop(0, m - 1, gather_sum, 0)

    def drain(step, c):
        x_copy(step).wait_send()
        for dist in range(tp_n - 1):
            for side in range(2):
                sends(side, step, dist, done)

        @pl.when(step < m - 1)
        def _():
            r_copy(step).wait_send()

        return c

    lax.fori_loop(0, m, drain, 0)
    over_peers(lambda p: a_copy(p).wait_send())
    over_peers(lambda p: a_arrival(p).wait_recv())


def finish(scale, gq_ref, gk_ref, gv_ref, gf_ref, gw_ref, oq_ref, ok_ref, ov_ref, of_ref, ow_ref, flat):
    ow_ref[...] = gw_ref[...] * scale
    oq_ref[...] = gq_ref[...]
    ok_ref[...] = gk_ref[...]
    ov_ref[...] = gv_ref[...]
    parts, halves, share, lanes = gf_ref.shape
    for h in range(halves):
        for part in range(parts):
            flat[part * share:(part + 1) * share, :] = gf_ref[part, h] * scale
        of_ref[h * lanes:(h + 1) * lanes, :] = flat[...].T


def body(ctx_n, tp_n, queries, key_proj, value_proj, filters, offsets, out_weight, out_grads):
    slab, chans = queries.shape
    taps = filters.shape[1]
    rows, features = out_grads.shape
    m = ctx_n // 2
    chunk = features // m
    oblk = features // ctx_n
    halves = chans // LANES
    share = taps // ctx_n
    grad_scale = float(ctx_n * slab) ** (-0.5)
    dma = pltpu.SemaphoreType.DMA
    vmem = pl.BlockSpec(memory_space=pltpu.VMEM)
    sds = jax.ShapeDtypeStruct
    gq, gk, gv, gf, gw = pl.pallas_call(
        functools.partial(kernel, ctx_n, tp_n),
        out_shape=(
            sds((slab, chans), BF16), sds((slab, chans), BF16), sds((slab, chans), BF16),
            sds((ctx_n, halves, share, LANES), F32), sds((oblk, chans), F32),
        ),
        in_specs=[pl.BlockSpec(memory_space=pl.ANY)] * 7,
        out_specs=(vmem,) * 5,
        scratch_shapes=[
            pltpu.VMEM((features, chans), BF16),
            pltpu.VMEM((m, slab, chunk), BF16),
            pltpu.VMEM((slab, chans), BF16),
            pltpu.VMEM((slab, chans), F32),
            pltpu.VMEM((slab, chans), F32),
            pltpu.VMEM((halves, slab + taps, LANES), F32),
            pltpu.VMEM((halves, slab + taps, LANES), F32),
            pltpu.VMEM((halves, taps, LANES), F32),
            pltpu.VMEM((slab, LANES), jnp.int32),
            pltpu.VMEM((slab, LANES), jnp.int32),
            pltpu.VMEM((taps, chans), BF16),
            pltpu.VMEM((taps, chans), BF16),
            pltpu.VMEM((taps, chans), BF16),
            pltpu.VMEM((taps, chans), BF16),
            pltpu.VMEM((chunk, chans), F32),
            pltpu.VMEM((m, oblk, chans), BF16),
            pltpu.VMEM((m, oblk, chans), BF16),
            pltpu.VMEM((m, oblk, chans), F32),
            pltpu.VMEM((m, oblk, chans), BF16),
            pltpu.VMEM((m, oblk, chans), BF16),
            pltpu.VMEM((ctx_n, halves, share, LANES), F32),
            pltpu.VMEM((ctx_n, halves, share, LANES), F32),
            pltpu.VMEM((halves, share, LANES), F32),
            pltpu.VMEM((slab, chans), BF16),
            pltpu.VMEM((slab, chans), BF16),
            pltpu.VMEM((slab, chans), BF16),
            pltpu.VMEM((chans, taps), F32),
            pltpu.VMEM((1, slab), jnp.int32),
            dma((5,)), dma((m,)), dma, dma((2, m, tp_n)), dma((2, m, tp_n)), dma, dma, dma, dma,
            dma((m,)), dma((m,)), dma((m,)), dma((m,)),
            dma((ctx_n,)), dma((ctx_n,)), dma((ctx_n,)), dma((ctx_n,)),
        ],
        compiler_params=pltpu.CompilerParams(
            collective_id=0, has_side_effects=True, vmem_limit_bytes=62 * 1024 * 1024
        ),
    )(queries, key_proj, value_proj, filters, offsets.reshape(1, slab), out_weight, out_grads)
    return pl.pallas_call(
        functools.partial(finish, grad_scale),
        out_shape=(
            sds((slab, chans), BF16), sds((slab, chans), BF16), sds((slab, chans), BF16),
            sds((chans, taps), F32), sds((oblk, chans), F32),
        ),
        in_specs=[vmem] * 5,
        out_specs=(vmem,) * 5,
        scratch_shapes=[pltpu.VMEM((taps, LANES), F32)],
    )(gq, gk, gv, gf, gw)


def solution(mesh):
    in_specs = (
        P("ctx", "tp"),
        P("ctx", "tp"),
        P("ctx", "tp"),
        P("tp", None),
        P("ctx"),
        P(None, "tp"),
        P(("ctx", "tp"), None),
    )
    out_specs = (P("ctx", "tp"), P("ctx", "tp"), P("ctx", "tp"), P("tp", None), P("ctx", "tp"))
    step = functools.partial(body, mesh.shape["ctx"], mesh.shape["tp"])
    return jax.shard_map(step, mesh=mesh, in_specs=in_specs, out_specs=out_specs, check_vma=False)
```

```python
import functools

import jax
import jax.numpy as jnp
from jax import lax
from jax.experimental import pallas as pl
from jax.experimental.pallas import tpu as pltpu
from jax.sharding import PartitionSpec as P

MESH = pl.DeviceIdType.MESH
F32 = jnp.float32
BF16 = jnp.bfloat16
LANES = 128
GROUP = 64
WIDTH = 8


def kernel(
    ctx_n, tp_n,
    q_hbm, k_hbm, v_hbm, f_hbm, off_hbm, w_hbm, og_ref,
    gq_ref, gk_ref, gv_ref, gf_ref, gw_ref,
    wbuf, gbuf, mixed, gm, filt, ext, gext, ft, capb, remb,
    psend, precv, hsend, hrecv, pbuf, xsend, xrecv, xown, rsend, rrecv,
    fg, frecv, fsum, q_ref, k_ref, v_ref, f_ref, off_ref,
    in_sem, og_sem, w_sem, gs_sem, gr_sem, ps_sem, pr_sem, hs_sem, hr_sem,
    xs_sem, xr_sem, rs_sem, rr_sem, fs_sem, fr_sem, as_sem, ar_sem,
):
    i = lax.axis_index("ctx")
    r = lax.axis_index("tp")
    slab, chans = q_ref.shape
    taps = f_ref.shape[1]
    rows, features = og_ref.shape
    m = ctx_n // 2
    chunk = features // m
    oblk = features // ctx_n
    halves = chans // LANES
    share = taps // ctx_n
    core = lax.rem(i, 2)
    chip = lax.div(i, 2)
    sibling = i + 1 - 2 * core

    barrier = pltpu.get_barrier_semaphore()

    def greet(p, c):
        pl.semaphore_signal(barrier, inc=1, device_id={"ctx": lax.rem(i + p, ctx_n), "tp": r}, device_id_type=MESH)
        return c

    lax.fori_loop(1, ctx_n, greet, 0)

    @pl.when(r > 0)
    def _():
        pl.semaphore_signal(barrier, inc=1, device_id={"ctx": i, "tp": r - 1}, device_id_type=MESH)

    @pl.when(r < tp_n - 1)
    def _():
        pl.semaphore_signal(barrier, inc=1, device_id={"ctx": i, "tp": r + 1}, device_id_type=MESH)

    def target(step):
        off = m - 1 - step
        high = lax.rem(lax.div(chip, 2) + lax.div(off, 2), m // 2)
        low = lax.rem(lax.rem(chip, 2) + lax.rem(off, 2), 2)
        return 2 * high + low

    own_rows = pl.ds(pl.multiple_of(r * rows, 16), rows)

    def own_columns(step):
        return og_ref.at[:, pl.ds(pl.multiple_of(target(step) * chunk, 128), chunk)]

    def place(step):
        return pltpu.make_async_copy(own_columns(step), gbuf.at[step, own_rows, :], og_sem.at[step])

    loads = [
        pltpu.make_async_copy(source, held, in_sem.at[n])
        for n, (source, held) in enumerate((
            (k_hbm, k_ref), (v_hbm, v_ref), (off_hbm, off_ref), (f_hbm, f_ref), (q_hbm, q_ref)
        ))
    ]
    for load in loads:
        load.start()

    def place_all(step, c):
        place(step).start()
        return c

    lax.fori_loop(0, m, place_all, 0)
    w_copy = pltpu.make_async_copy(w_hbm, wbuf, w_sem)
    w_copy.start()
    nbrs = jnp.where(r > 0, 1, 0) + jnp.where(r < tp_n - 1, 1, 0)
    pl.semaphore_wait(barrier, ctx_n - 1 + nbrs)

    def gather_copy(side, step, dist, source, dest):
        window = gbuf.at[step, pl.ds(pl.multiple_of(source * rows, 16), rows), :]
        return pltpu.make_async_remote_copy(
            src_ref=own_columns(step) if dist == 0 else window, dst_ref=window,
            send_sem=gs_sem.at[side, step, dist], recv_sem=gr_sem.at[side, step, dist],
            device_id={"ctx": i, "tp": dest}, device_id_type=MESH,
        )

    def sends(side, step, dist, act):
        if side == 0:
            cond = (r - dist >= 0) & (r + 1 < tp_n)
            source, dest = r - dist, r + 1
        else:
            cond = (r + dist < tp_n) & (r >= 1)
            source, dest = r + dist, r - 1

        @pl.when(cond)
        def _():
            act(gather_copy(side, step, dist, source, dest))

    def arrives(side, step, dist):
        if side == 0:
            cond, source = r - 1 - dist >= 0, r - 1 - dist
            dest = r - 1
        else:
            cond, source = r + 1 + dist < tp_n, r + 1 + dist
            dest = r + 1

        @pl.when(cond)
        def _():
            gather_copy(side, step, dist, source, dest).wait_recv()

    def start(c):
        c.start()

    def done(c):
        c.wait_send()

    for step in range(min(2, m)):
        for side in range(2):
            sends(side, step, 0, start)


    loads[0].wait()
    loads[1].wait()
    product = (k_ref[...].astype(F32) * v_ref[...].astype(F32)).astype(BF16)
    psend[...] = product[slab - taps:, :]
    p_copy = pltpu.make_async_remote_copy(
        src_ref=psend, dst_ref=precv, send_sem=ps_sem, recv_sem=pr_sem,
        device_id={"ctx": lax.rem(i + 1, ctx_n), "tp": r}, device_id_type=MESH,
    )
    p_copy.start()
    for h in range(halves):
        ext[h, taps:, :] = product[:, h * LANES:(h + 1) * LANES].astype(F32)
    loads[2].wait()
    loads[3].wait()
    for h in range(halves):
        ft[h] = f_ref[h * LANES:(h + 1) * LANES, :].T

    lane_tok = lax.broadcasted_iota(jnp.int32, (slab, slab), 1)
    row_tok = lax.broadcasted_iota(jnp.int32, (slab, slab), 0)
    offs = jnp.broadcast_to(off_ref[...], (slab, slab))
    off_col = jnp.sum(jnp.where(lane_tok == row_tok, offs, 0).astype(F32), axis=1, keepdims=True)
    later = jnp.where((lane_tok > row_tok) & (offs == 0), lane_tok - row_tok - 1, taps - 1)
    rem_col = jnp.min(later.astype(F32), axis=1, keepdims=True)
    capb[...] = jnp.broadcast_to(off_col, (slab, LANES)).astype(jnp.int32)
    remb[...] = jnp.broadcast_to(jnp.minimum(rem_col, taps - 1), (slab, LANES)).astype(jnp.int32)
    gm[...] = jnp.zeros_like(gm)

    def tap_sum(source, base_row, sign, caps, emit):
        for g in range(slab // GROUP):
            t0 = g * GROUP
            cap = caps[t0:t0 + GROUP, :]

            def block(b, acc):
                acc = list(acc)
                for s in range(WIDTH):
                    j = b * WIDTH + s
                    keep = cap >= j
                    for h in range(halves):
                        window = source[h, pl.ds(base_row + t0 + sign * j, GROUP), :]
                        coeff = ft[h, pl.ds(j, 1), :]
                        acc[h] = acc[h] + jnp.where(keep, window * coeff, 0.0)
                return tuple(acc)

            zero = tuple(jnp.zeros((GROUP, LANES), F32) for _ in range(halves))
            acc = lax.fori_loop(0, taps // WIDTH, block, zero)
            for h in range(halves):
                emit(t0, h, acc[h])

    def emit_forward(t0, h, value):
        span, cols = slice(t0, t0 + GROUP), slice(h * LANES, (h + 1) * LANES)
        filt[span, cols] = value
        mixed[span, cols] = (q_ref[span, cols].astype(F32) * value).astype(BF16)

    def forward_taps():
        loads[4].wait()
        p_copy.wait()
        earlier = jnp.where(i > 0, precv[...].astype(F32), 0.0)
        for h in range(halves):
            ext[h, :taps, :] = earlier[:, h * LANES:(h + 1) * LANES]
        tap_sum(ext, taps, -1, capb, emit_forward)
        w_copy.wait()

    def x_copy(step):
        return pltpu.make_async_remote_copy(
            src_ref=xsend.at[step], dst_ref=xrecv.at[step],
            send_sem=xs_sem.at[step], recv_sem=xr_sem.at[step],
            device_id={"ctx": sibling, "tp": r}, device_id_type=MESH,
        )

    def r_copy(step):
        return pltpu.make_async_remote_copy(
            src_ref=rsend.at[step], dst_ref=rrecv.at[step],
            send_sem=rs_sem.at[step], recv_sem=rr_sem.at[step],
            device_id={"ctx": 2 * target(step) + core, "tp": r}, device_id_type=MESH,
        )

    def forward_pair(step):
        x_copy(step).wait_recv()
        rsend[step] = (xown[step] + xrecv[step].astype(F32)).astype(BF16)
        r_copy(step).start()

    lag = tp_n - 2

    def compute(step):
        @pl.when(step > 0)
        def _():
            forward_pair(step - 1)

        place(step).wait()
        block = gbuf[step]
        pbuf[...] = lax.dot_general(block, mixed[...], (((0,), (0,)), ((), ())), preferred_element_type=F32)
        xsend[step] = pbuf[pl.ds(pl.multiple_of((1 - core) * oblk, 16), oblk), :].astype(BF16)
        x_copy(step).start()
        xown[step] = pbuf[pl.ds(pl.multiple_of(core * oblk, 16), oblk), :]
        span = pl.ds(pl.multiple_of(target(step) * chunk, 128), chunk)
        gm[...] += jnp.dot(block, wbuf[span, :], preferred_element_type=F32)

    def main(turn, c):
        @pl.when(turn + 2 < m)
        def _():
            for side in range(2):
                sends(side, turn + 2, 0, start)

        for dist in range(tp_n - 1):
            step = turn - dist

            @pl.when((step >= 0) & (step < m))
            def _():
                for side in range(2):
                    arrives(side, step, dist)
                    if dist + 1 < tp_n - 1:
                        sends(side, step, dist + 1, start)

        @pl.when(turn == 0)
        def _():
            forward_taps()

        @pl.when(turn >= lag)
        def _():
            compute(turn - lag)

        return c

    lax.fori_loop(0, m + lag, main, 0)

    q_wide = q_ref[...].astype(F32)
    grad_mixed = gm[...]
    grad_filtered = (grad_mixed * q_wide).astype(BF16)
    wide = grad_filtered.astype(F32)
    lead_tok = lax.broadcasted_iota(jnp.int32, (taps, LANES), 0)
    for h in range(halves):
        part = wide[:, h * LANES:(h + 1) * LANES]
        gext[h, :slab, :] = part
        lead = jnp.where(capb[:taps, :] > lead_tok, part[:taps], 0.0)
        hsend[:, h * LANES:(h + 1) * LANES] = lead.astype(BF16)
    h_copy = pltpu.make_async_remote_copy(
        src_ref=hsend, dst_ref=hrecv, send_sem=hs_sem, recv_sem=hr_sem,
        device_id={"ctx": lax.rem(i + ctx_n - 1, ctx_n), "tp": r}, device_id_type=MESH,
    )
    h_copy.start()
    gq_ref[...] = (grad_mixed * filt[...]).astype(BF16)

    def tap_columns(b, c):
        for s in range(WIDTH):
            j = b * WIDTH + s
            total = [jnp.zeros((8, LANES), F32) for _ in range(halves)]
            for g in range(slab // GROUP):
                t0 = g * GROUP
                keep = capb[t0:t0 + GROUP, :] >= j
                for h in range(halves):
                    window = ext[h, pl.ds(taps + t0 - j, GROUP), :]
                    term = jnp.where(keep, window * gext[h, t0:t0 + GROUP, :], 0.0)
                    total[h] = total[h] + jnp.sum(term.reshape(GROUP // 8, 8, LANES), axis=0)
            for h in range(halves):
                fg[lax.div(j, share), h, pl.ds(lax.rem(j, share), 1), :] = jnp.sum(total[h], axis=0, keepdims=True)
        return c

    lax.fori_loop(0, taps // WIDTH, tap_columns, 0)

    def f_copy(p):
        peer = lax.rem(i + p, ctx_n)
        return pltpu.make_async_remote_copy(
            src_ref=fg.at[peer], dst_ref=frecv.at[p], send_sem=fs_sem.at[p], recv_sem=fr_sem.at[p],
            device_id={"ctx": peer, "tp": r}, device_id_type=MESH,
        )

    def a_copy(p):
        return pltpu.make_async_remote_copy(
            src_ref=fsum, dst_ref=gf_ref.at[i], send_sem=as_sem.at[p], recv_sem=ar_sem.at[p],
            device_id={"ctx": lax.rem(i + p, ctx_n), "tp": r}, device_id_type=MESH,
        )

    def a_arrival(p):
        source = lax.rem(i + ctx_n - p, ctx_n)
        return pltpu.make_async_remote_copy(
            src_ref=fsum, dst_ref=gf_ref.at[source], send_sem=as_sem.at[p], recv_sem=ar_sem.at[p],
            device_id={"ctx": source, "tp": r}, device_id_type=MESH,
        )

    def over_peers(act):
        def one(p, c):
            act(p)
            return c

        lax.fori_loop(1, ctx_n, one, 0)

    over_peers(lambda p: f_copy(p).start())

    h_copy.wait()
    follow = jnp.where(i < ctx_n - 1, hrecv[...].astype(F32), 0.0)
    for h in range(halves):
        gext[h, slab:, :] = follow[:, h * LANES:(h + 1) * LANES]

    def emit_backward(t0, h, value):
        span, cols = slice(t0, t0 + GROUP), slice(h * LANES, (h + 1) * LANES)
        gk_ref[span, cols] = (value * v_ref[span, cols].astype(F32)).astype(BF16)
        gv_ref[span, cols] = (value * k_ref[span, cols].astype(F32)).astype(BF16)

    over_peers(lambda p: f_copy(p).wait())
    frecv[0] = fg[i]
    fsum[...] = jnp.sum(frecv[...], axis=0)
    gf_ref[i] = fsum[...]
    over_peers(lambda p: a_copy(p).start())

    tap_sum(gext, 0, 1, remb, emit_backward)

    last = m - 1
    x_copy(last).wait_recv()
    gw_ref[...] = xown[last] + xrecv[last].astype(F32)

    def gather_sum(step, c):
        r_copy(step).wait_recv()
        gw_ref[...] += rrecv[step].astype(F32)
        return c

    lax.fori_loop(0, m - 1, gather_sum, 0)

    def drain(step, c):
        x_copy(step).wait_send()
        for dist in range(tp_n - 1):
            for side in range(2):
                sends(side, step, dist, done)

        @pl.when(step < m - 1)
        def _():
            r_copy(step).wait_send()

        return c

    lax.fori_loop(0, m, drain, 0)
    over_peers(lambda p: a_copy(p).wait_send())
    over_peers(lambda p: a_arrival(p).wait_recv())


def finish(scale, gq_ref, gk_ref, gv_ref, gf_ref, gw_ref, oq_ref, ok_ref, ov_ref, of_ref, ow_ref, flat):
    ow_ref[...] = gw_ref[...] * scale
    oq_ref[...] = gq_ref[...]
    ok_ref[...] = gk_ref[...]
    ov_ref[...] = gv_ref[...]
    parts, halves, share, lanes = gf_ref.shape
    for h in range(halves):
        for part in range(parts):
            flat[part * share:(part + 1) * share, :] = gf_ref[part, h] * scale
        of_ref[h * lanes:(h + 1) * lanes, :] = flat[...].T


def body(ctx_n, tp_n, queries, key_proj, value_proj, filters, offsets, out_weight, out_grads):
    slab, chans = queries.shape
    taps = filters.shape[1]
    rows, features = out_grads.shape
    m = ctx_n // 2
    chunk = features // m
    oblk = features // ctx_n
    halves = chans // LANES
    share = taps // ctx_n
    grad_scale = float(ctx_n * slab) ** (-0.5)
    dma = pltpu.SemaphoreType.DMA
    vmem = pl.BlockSpec(memory_space=pltpu.VMEM)
    sds = jax.ShapeDtypeStruct
    gq, gk, gv, gf, gw = pl.pallas_call(
        functools.partial(kernel, ctx_n, tp_n),
        out_shape=(
            sds((slab, chans), BF16), sds((slab, chans), BF16), sds((slab, chans), BF16),
            sds((ctx_n, halves, share, LANES), F32), sds((oblk, chans), F32),
        ),
        in_specs=[pl.BlockSpec(memory_space=pl.ANY)] * 7,
        out_specs=(vmem,) * 5,
        scratch_shapes=[
            pltpu.VMEM((features, chans), BF16),
            pltpu.VMEM((m, slab, chunk), BF16),
            pltpu.VMEM((slab, chans), BF16),
            pltpu.VMEM((slab, chans), F32),
            pltpu.VMEM((slab, chans), F32),
            pltpu.VMEM((halves, slab + taps, LANES), F32),
            pltpu.VMEM((halves, slab + taps, LANES), F32),
            pltpu.VMEM((halves, taps, LANES), F32),
            pltpu.VMEM((slab, LANES), jnp.int32),
            pltpu.VMEM((slab, LANES), jnp.int32),
            pltpu.VMEM((taps, chans), BF16),
            pltpu.VMEM((taps, chans), BF16),
            pltpu.VMEM((taps, chans), BF16),
            pltpu.VMEM((taps, chans), BF16),
            pltpu.VMEM((chunk, chans), F32),
            pltpu.VMEM((m, oblk, chans), BF16),
            pltpu.VMEM((m, oblk, chans), BF16),
            pltpu.VMEM((m, oblk, chans), F32),
            pltpu.VMEM((m, oblk, chans), BF16),
            pltpu.VMEM((m, oblk, chans), BF16),
            pltpu.VMEM((ctx_n, halves, share, LANES), F32),
            pltpu.VMEM((ctx_n, halves, share, LANES), F32),
            pltpu.VMEM((halves, share, LANES), F32),
            pltpu.VMEM((slab, chans), BF16),
            pltpu.VMEM((slab, chans), BF16),
            pltpu.VMEM((slab, chans), BF16),
            pltpu.VMEM((chans, taps), F32),
            pltpu.VMEM((1, slab), jnp.int32),
            dma((5,)), dma((m,)), dma, dma((2, m, tp_n)), dma((2, m, tp_n)), dma, dma, dma, dma,
            dma((m,)), dma((m,)), dma((m,)), dma((m,)),
            dma((ctx_n,)), dma((ctx_n,)), dma((ctx_n,)), dma((ctx_n,)),
        ],
        compiler_params=pltpu.CompilerParams(
            collective_id=0, has_side_effects=True, vmem_limit_bytes=62 * 1024 * 1024
        ),
    )(queries, key_proj, value_proj, filters, offsets.reshape(1, slab), out_weight, out_grads)
    return pl.pallas_call(
        functools.partial(finish, grad_scale),
        out_shape=(
            sds((slab, chans), BF16), sds((slab, chans), BF16), sds((slab, chans), BF16),
            sds((chans, taps), F32), sds((oblk, chans), F32),
        ),
        in_specs=[vmem] * 5,
        out_specs=(vmem,) * 5,
        scratch_shapes=[pltpu.VMEM((taps, LANES), F32)],
    )(gq, gk, gv, gf, gw)


def solution(mesh):
    in_specs = (
        P("ctx", "tp"),
        P("ctx", "tp"),
        P("ctx", "tp"),
        P("tp", None),
        P("ctx"),
        P(None, "tp"),
        P(("ctx", "tp"), None),
    )
    out_specs = (P("ctx", "tp"), P("ctx", "tp"), P("ctx", "tp"), P("tp", None), P("ctx", "tp"))
    step = functools.partial(body, mesh.shape["ctx"], mesh.shape["tp"])
    return jax.shard_map(step, mesh=mesh, in_specs=in_specs, out_specs=out_specs, check_vma=False)
```
